128 devices in a mesh: member: 4 (over z_hi, core), space: 32 (over y, x, z_lo).
Axes of the slice: x: 4, y: 4, z: 4 (z_hi: 2, z_lo: 2; z = z_hi * 2 + z_lo), core: 2. Of those that a mesh axis runs over, the one named last changes fastest.
Arguments:
- trajectory_outcomes: float32 [8, 96, 131072], P('member', None, 'space'), may hold values from -8 to 8
- verifying_analysis: float32 [96, 131072], P(None, 'space'), may hold values from -8 to 8
- latitude_surface_factor: float32 [131072], P('space'), may hold values from 0.5 to 6, as said below
- variable_penalty_factor: float32 [96], replicated, may hold values from 0.25 to 4
Outputs:
- derivative_by_trajectory: float32 [8, 96, 131072], P('member', None, 'space')
- field_loss: float32 [96], replicated
The draws below stay inside these ranges and needn't reach their ends.
Inputs may be any that keep to these rules, and one draw needn't show every extreme that they name: `latitude_surface_factor`: positive area weights.
All inputs are finite; a program needn't handle non-finite values.
Results may differ from the reference program's by a relative error of at most 0.0003.
Values sent between devices are 32-bit elements; how exact they have to be, the bound alone decides.
No kernel may reach another device: no remote copies, remote signals or barrier semaphores. Data moves between devices by JAX's collectives and lax.ppermute only.
A program may use at most 128 MiB of HBM per device.

```python
import math
import jax
import jax.numpy as jnp

QUANTITY_TALLY = 96
TRAJECTORY_TALLY = 8
MESH_NODE_TALLY = 131072


def shared_ensemble(key, center_scale, spacing_low, spacing_high):
    key_order, key_jitter, key_center, key_spacing = jax.random.split(key, 4)
    slots = TRAJECTORY_TALLY + 1
    scores = jax.random.randint(key_order, (slots, QUANTITY_TALLY, MESH_NODE_TALLY), 0, 2 ** 20) * 16 + jnp.arange(slots, dtype=jnp.int32)[:, None, None]
    ordering = jnp.argsort(jnp.argsort(scores, axis=0), axis=0).astype(jnp.float32)
    jitter = jax.random.uniform(key_jitter, (slots, QUANTITY_TALLY, MESH_NODE_TALLY), jnp.float32, -0.3, 0.3)
    center = jax.random.uniform(key_center, (QUANTITY_TALLY, MESH_NODE_TALLY), jnp.float32, -1.0, 1.0) * center_scale
    spacing = jnp.exp(jax.random.uniform(key_spacing, (QUANTITY_TALLY, MESH_NODE_TALLY), jnp.float32, math.log(spacing_low), math.log(spacing_high)))
    middle = 0.5 * (slots - 1)
    return center[None] + spacing[None] * (ordering - middle + jitter)


def draw_trajectory_outcomes(key, part):
    values = shared_ensemble(key, 1.5, 0.2, 0.8)
    return values[:TRAJECTORY_TALLY]


def draw_verifying_analysis(key, part):
    values = shared_ensemble(key, 1.5, 0.2, 0.8)
    return values[TRAJECTORY_TALLY]


def draw_latitude_surface_factor(key, part):
    key = jax.random.fold_in(key, 7)
    position = jnp.arange(MESH_NODE_TALLY, dtype=jnp.float32) / MESH_NODE_TALLY
    roughness = jnp.exp(jax.random.uniform(key, (MESH_NODE_TALLY,), jnp.float32, math.log(0.5), math.log(2.0)))
    return (1.0 + 2.0 * position) * roughness


def setup_inputs(seed: int = 0) -> dict:
    key_list = jax.random.split(jax.random.key(seed), 5)
    trajectory_outcomes = draw_trajectory_outcomes(jax.random.fold_in(key_list[4], 71), 0)
    verifying_analysis = draw_verifying_analysis(jax.random.fold_in(key_list[4], 71), 0)
    latitude_surface_factor = draw_latitude_surface_factor(jax.random.fold_in(key_list[4], 71), 0)
    variable_penalty_factor = jnp.clip(jnp.exp(jax.random.uniform(key_list[3], (QUANTITY_TALLY,), jnp.float32, math.log(0.25), math.log(4.0))), 0.25, 4.0)
    return {"trajectory_outcomes": trajectory_outcomes, "verifying_analysis": verifying_analysis, "latitude_surface_factor": latitude_surface_factor, "variable_penalty_factor": variable_penalty_factor}


def reference(trajectory_outcomes, verifying_analysis, latitude_surface_factor, variable_penalty_factor):
    trajectory_samples = trajectory_outcomes.shape[0]
    pairwise_multiplier = (1.0 - 0.05 / trajectory_samples) / (trajectory_samples * (trajectory_samples - 1))
    error_versus_truth = trajectory_outcomes - verifying_analysis[None]
    running_sign_sum = [jnp.zeros(verifying_analysis.shape, jnp.float32) for former_sample in range(trajectory_samples)]
    dispersion_term = jnp.zeros(verifying_analysis.shape, jnp.float32)
    for former_sample in range(trajectory_samples):
        for latter_sample in range(former_sample + 1, trajectory_samples):
            realization_gap = trajectory_outcomes[former_sample] - trajectory_outcomes[latter_sample]
            pair_sign = jnp.sign(realization_gap)
            running_sign_sum[former_sample] = running_sign_sum[former_sample] + pair_sign
            running_sign_sum[latter_sample] = running_sign_sum[latter_sample] - pair_sign
            dispersion_term = dispersion_term + 2.0 * jnp.abs(realization_gap)
    scaling_coefficient = variable_penalty_factor[None, :, None] * latitude_surface_factor[None, None, :]
    derivative_by_trajectory = scaling_coefficient * (jnp.sign(error_versus_truth) / trajectory_samples - pairwise_multiplier * jnp.stack(running_sign_sum))
    per_node_score = jnp.sum(jnp.abs(error_versus_truth), axis=0) / trajectory_samples - 0.5 * pairwise_multiplier * dispersion_term
    field_loss = variable_penalty_factor * jnp.sum(per_node_score * latitude_surface_factor[None], axis=1) / MESH_NODE_TALLY
    return derivative_by_trajectory, field_loss
```

```python
import functools

import jax
import jax.numpy as jnp
from jax import lax
from jax.experimental import pallas as pl
from jax.experimental.pallas import tpu as pltpu
from jax.sharding import PartitionSpec as P

AXES = ("member", "space")
CHUNKS = 2
LANES = 128
SUBLANES = 8


def exchange(block, flip):
    members, spaces = lax.axis_size("member"), lax.axis_size("space")
    pairs = [
        (m * spaces + s, (m ^ flip) * spaces + s) for m in range(members) for s in range(spaces)
    ]
    return lax.ppermute(block, AXES, pairs)


def score_kernel(scale, weight, own, near, far, cross, truth, lat, pen, d_own, d_near, d_far, d_cross, loss):
    rows, cols = truth.shape
    sources = (own, near, far, cross)
    targets = (d_own, d_near, d_far, d_cross)
    for row in range(0, rows, SUBLANES):
        r = pl.ds(row, SUBLANES)
        penalty = pen[r, :]

        def step(i, total):
            c = pl.ds(pl.multiple_of(i * LANES, LANES), LANES)
            x = [ref[k, r, c] for ref in sources for k in range(2)]
            n = len(x)
            y = truth[r, c]
            area = jnp.broadcast_to(lat[:, c], (SUBLANES, LANES))
            signs = [None] * n
            for a in range(n):
                for b in range(a + 1, n):
                    s = jnp.where(x[a] > x[b], 1.0, jnp.where(x[a] < x[b], -1.0, 0.0))
                    signs[a] = s if signs[a] is None else signs[a] + s
                    signs[b] = -s if signs[b] is None else signs[b] - s
            factor = penalty * area
            score = jnp.zeros_like(y)
            for j in range(n):
                e = x[j] - y
                g = jnp.where(e > 0.0, weight, jnp.where(e < 0.0, -weight, 0.0)) - scale * signs[j]
                score = score + e * g
                targets[j // 2][j % 2, r, c] = factor * g
            return total + area * score

        total = lax.fori_loop(0, cols // LANES, step, jnp.zeros((SUBLANES, LANES), jnp.float32), unroll=2)
        loss[r, :] = total


def shards(x, y, lat, pen):
    members = lax.axis_size("member")
    spaces = lax.axis_size("space")
    samples = x.shape[0] * members
    fields, points = y.shape
    scale = (1.0 - 0.05 / samples) / (samples * (samples - 1))
    quarter = fields // members
    width = points // CHUNKS
    me = lax.axis_index("member")

    def part(array, flip, chunk):
        start = ((me ^ flip) * quarter, chunk * width)
        size = (quarter, width)
        if array.ndim == 3:
            start, size = (0,) + start, (array.shape[0],) + size
        return lax.dynamic_slice(array, start, size)

    got = [{f: exchange(part(x, f, c), f) for f in (2, 3, 1)} for c in range(CHUNKS)]
    pen_own = lax.dynamic_slice(pen, (me * quarter,), (quarter,))
    pen_own = jnp.broadcast_to(pen_own[:, None], (quarter, LANES))
    block = jax.ShapeDtypeStruct((x.shape[0], quarter, width), jnp.float32)
    vmem = pl.BlockSpec(memory_space=pltpu.VMEM)
    call = pl.pallas_call(
        functools.partial(score_kernel, scale, 1.0 / samples),
        out_shape=[block] * 4 + [jax.ShapeDtypeStruct((quarter, LANES), jnp.float32)],
        in_specs=[vmem] * 7,
        out_specs=[vmem] * 5,
        compiler_params=pltpu.CompilerParams(vmem_limit_bytes=32 * 1024 * 1024),
        cost_estimate=pl.CostEstimate(
            flops=300 * quarter * width, bytes_accessed=20 * quarter * width * 4, transcendentals=0
        ),
    )
    pieces = []
    loss = 0.0
    for c in range(CHUNKS):
        d_own, d_near, d_far, d_cross, part_loss = call(
            part(x, 0, c), got[c][1], got[c][2], got[c][3], part(y, 0, c),
            lat[None, c * width:(c + 1) * width], pen_own,
        )
        loss = loss + part_loss
        pieces.append({0: d_own, 2: exchange(d_far, 2), 3: exchange(d_cross, 3), 1: exchange(d_near, 1)})
    sums = jnp.sum(loss, axis=1)[None, :]
    devices = members * spaces
    everyone = lax.all_to_all(jnp.broadcast_to(sums[None], (devices,) + sums.shape), AXES, 0, 0)
    total = jnp.sum(everyone.reshape(members, spaces, quarter), axis=1).reshape(fields)
    field_loss = pen * total / (points * spaces)
    out = jnp.zeros(x.shape, jnp.float32)
    for c in range(CHUNKS):
        for f in (0, 1, 2, 3):
            out = lax.dynamic_update_slice(out, pieces[c][f], (0, (me ^ f) * quarter, c * width))
    return out, field_loss


def solution(mesh):
    return jax.shard_map(
        shards,
        mesh=mesh,
        in_specs=(P("member", None, "space"), P(None, "space"), P("space"), P()),
        out_specs=(P("member", None, "space"), P()),
        check_vma=False,
    )
```

```python
import functools
import math

import jax
import jax.numpy as jnp
from jax import lax
from jax.experimental import pallas as pl
from jax.experimental.pallas import tpu as pltpu
from jax.sharding import PartitionSpec as P

AXES = ("member", "space")
SPLIT = 0.625
LANES = 128
SUBLANES = 8
NEAR, FAR, CROSS = 1, 2, 3
SMALL, LARGE = 4 * 2**20, 16 * 2**20
WORK, PLACING = 400_000, 40 * 10**9
VMEM = pl.BlockSpec(memory_space=pltpu.VMEM)
HBM = pl.BlockSpec(memory_space=pltpu.HBM)
ANY = pl.BlockSpec(memory_space=pl.ANY)


def exchange(block, flip):
    members, spaces = lax.axis_size("member"), lax.axis_size("space")
    pairs = [
        (m * spaces + s, (m ^ flip) * spaces + s) for m in range(members) for s in range(spaces)
    ]
    return lax.ppermute(block, AXES, pairs)


def window(ref, flip, quarter, start, width):
    row = pl.multiple_of((lax.axis_index("member") ^ flip) * quarter, SUBLANES)
    index = (pl.ds(row, quarter), pl.ds(start, width))
    return ref.at[(slice(None),) + index if len(ref.shape) == 3 else index]


def moved(shapes, flops=0):
    size = sum(4 * math.prod(s) for s in shapes)
    return pl.CostEstimate(flops=flops, bytes_accessed=2 * size, transcendentals=0)


def take_kernel(specs, quarter, n_arrays, n_deps, *refs):
    arrays, outs, sems = refs[:n_arrays], refs[n_arrays + n_deps:-1], refs[-1]
    copies = []
    for i, (which, flip, start, width) in enumerate(specs):
        source = window(arrays[which], flip, quarter, start, width)
        copies.append(pltpu.make_async_copy(source, outs[i], sems.at[i]))
    for copy in copies:
        copy.start()
    for copy in copies:
        copy.wait()


def take(specs, quarter, arrays, deps=()):
    shapes = [arrays[w].shape[:-2] + (quarter, width) for w, _, _, width in specs]
    return pl.pallas_call(
        functools.partial(take_kernel, specs, quarter, len(arrays), len(deps)),
        out_shape=[jax.ShapeDtypeStruct(s, jnp.float32) for s in shapes],
        in_specs=[HBM] * len(arrays) + [ANY] * len(deps),
        out_specs=[VMEM] * len(specs),
        scratch_shapes=[pltpu.SemaphoreType.DMA((len(specs),))],
        compiler_params=pltpu.CompilerParams(vmem_limit_bytes=SMALL),
        cost_estimate=moved(shapes),
    )(*[pltpu.with_memory_space_constraint(a, pltpu.HBM) for a in arrays], *deps)


def place_kernel(specs, quarter, job, n_more, *refs):
    pieces, more, outs, sems = refs[:len(specs)], refs[len(specs) + 1:][:n_more], refs[len(specs) + 1 + n_more:-1], refs[-1]
    copies = []
    for i, (flip, start, width) in enumerate(specs):
        copies.append(pltpu.make_async_copy(pieces[i], window(outs[0], flip, quarter, start, width), sems.at[i]))
    for copy in copies:
        copy.start()
    if job is not None:
        small = outs[2]
        job(*more, small)
        copies.append(pltpu.make_async_copy(small, outs[1], sems.at[len(specs)]))
        copies[-1].start()
    for copy in copies:
        copy.wait()


def place(specs, quarter, pieces, out, flops=0, job=None, more=(), shape=None):
    shapes = [out.shape] + ([shape] if job else [])
    return pl.pallas_call(
        functools.partial(place_kernel, specs, quarter, job, len(more)),
        out_shape=[jax.ShapeDtypeStruct(s, jnp.float32) for s in shapes],
        in_specs=[VMEM] * len(pieces) + [HBM] + [VMEM] * len(more),
        out_specs=[HBM] * len(shapes),
        scratch_shapes=[pltpu.VMEM(s, jnp.float32) for s in shapes[1:]] + [pltpu.SemaphoreType.DMA((len(specs) + 1,))],
        input_output_aliases={len(pieces): 0},
        compiler_params=pltpu.CompilerParams(vmem_limit_bytes=SMALL),
        cost_estimate=moved([p.shape for p in pieces], flops),
    )(*pieces, out, *more)


def add_rows(rows, total):
    total[...] = jnp.sum(rows[:, 0, :], axis=0, keepdims=True)


def weigh(count, pen, own, far, cross, near, loss):
    total = own[...] + far[...] + cross[...] + near[...]
    loss[...] = pen[...] * total[:, :pen.shape[1]] / count


def score_kernel(scale, weight, start, last, n_before, own, near, far, cross, truth, lat, pen, *refs):
    before, refs = refs[:n_before], refs[n_before:]
    far_out, cross_out, d_near, loss, out, row_sums, d_own, d_far, d_cross, sems = refs
    rows, cols = d_far.shape[1:]
    sources = ((own, start), (near, start), (far, 0), (cross, 0))
    targets = ((d_own, 0), (d_near, start), (d_far, 0), (d_cross, 0))
    homes = ((d_own, window(out, 0, rows, start, cols)), (d_far, far_out), (d_cross, cross_out))
    copies = []
    for row in range(0, rows, SUBLANES):
        r = pl.ds(row, SUBLANES)
        penalty = pen[pl.ds(pl.multiple_of(lax.axis_index("member") * rows + row, SUBLANES), SUBLANES), :]

        def step(i, total):
            def at(shift):
                return pl.ds(pl.multiple_of(i * LANES + shift, LANES), LANES)

            x = [ref[k, r, at(shift)] for ref, shift in sources for k in range(2)]
            n = len(x)
            y = truth[r, at(start)]
            area = jnp.broadcast_to(lat[:, at(start)], (SUBLANES, LANES))
            signs = [None] * n
            for a in range(n):
                for b in range(a + 1, n):
                    s = jnp.where(x[a] > x[b], 1.0, jnp.where(x[a] < x[b], -1.0, 0.0))
                    signs[a] = s if signs[a] is None else signs[a] + s
                    signs[b] = -s if signs[b] is None else signs[b] - s
            factor = penalty * area
            score = jnp.zeros_like(y)
            for j in range(n):
                e = x[j] - y
                g = jnp.where(e > 0.0, weight, jnp.where(e < 0.0, -weight, 0.0)) - scale * signs[j]
                score = score + e * g
                target, shift = targets[j // 2]
                target[j % 2, r, at(shift)] = factor * g
            return total + area * score

        total = before[1][r, :] if before else jnp.zeros((SUBLANES, LANES), jnp.float32)
        total = lax.fori_loop(0, cols // LANES, step, total, unroll=2)
        loss[r, :] = total
        for i, (source, home) in enumerate(homes):
            copies.append(pltpu.make_async_copy(source.at[:, r], home.at[:, r], sems.at[i, row // SUBLANES]))
            copies[-1].start()
    if last:
        sums = jnp.sum(loss[...], axis=1, keepdims=True)
        field = lax.axis_index("member") * rows + lax.broadcasted_iota(jnp.int32, loss.shape, 0)
        here = lax.broadcasted_iota(jnp.int32, loss.shape, 1) == field
        row_sums[...] = jnp.sum(jnp.where(here, sums, 0.0), axis=0, keepdims=True)
    for copy in copies:
        copy.wait()


def score(scale, weight, start, width, shape, last, own, near, far, cross, truth, lat, pen, *before):
    members, quarter = own.shape[:2]
    block = (members, quarter, width)
    shapes = (block, block, own.shape, (quarter, LANES), shape, (1, LANES))
    return pl.pallas_call(
        functools.partial(score_kernel, scale, weight, start, last, len(before)),
        out_shape=[jax.ShapeDtypeStruct(s, jnp.float32) for s in shapes],
        in_specs=[VMEM] * 7 + [VMEM, VMEM, HBM][:len(before)],
        out_specs=[HBM, HBM, VMEM, VMEM, HBM, VMEM],
        scratch_shapes=[pltpu.VMEM(block, jnp.float32)] * 3 + [pltpu.SemaphoreType.DMA((3, quarter // SUBLANES))],
        input_output_aliases={7: 2, 8: 3, 9: 4} if before else {},
        compiler_params=pltpu.CompilerParams(vmem_limit_bytes=LARGE),
        cost_estimate=pl.CostEstimate(
            flops=WORK * quarter * width, bytes_accessed=20 * quarter * width * 4, transcendentals=0
        ),
    )(own, near, far, cross, truth, lat, pen, *before)


def shards(x, y, lat, pen):
    members = lax.axis_size("member")
    spaces = lax.axis_size("space")
    samples = x.shape[0] * members
    fields, points = y.shape
    scale = (1.0 - 0.05 / samples) / (samples * (samples - 1))
    quarter = fields // members
    first = int(points * SPLIT)
    chunks = ((0, first), (first, points - first))

    far_cross = [[(0, FAR, start, width), (0, CROSS, start, width)] for start, width in chunks]
    to_near, *first_sent = take([(0, NEAR, 0, points)] + far_cross[0], quarter, [x])
    second_sent = take(far_cross[1], quarter, [x], first_sent)
    own, truth = take([(0, 0, 0, points), (1, 0, 0, points)], quarter, [x, y], second_sent)
    sent = (first_sent, second_sent)
    far = [exchange(pair[0], FAR) for pair in sent]
    cross = [exchange(pair[1], CROSS) for pair in sent]
    near = exchange(to_near, NEAR)
    pen_lanes = jnp.broadcast_to(pen[:, None], (fields, LANES))
    back, before = [], ()
    for c, (start, width) in enumerate(chunks):
        d_far, d_cross, *before, sums = score(
            scale, 1.0 / samples, start, width, x.shape, c == len(chunks) - 1, own, near, far[c], cross[c], truth, lat[None, :], pen_lanes, *before
        )
        back.append([(FAR, start, width, exchange(d_far, FAR)), (CROSS, start, width, exchange(d_cross, CROSS))])
    d_near, loss, out = before
    back.insert(1, [(NEAR, 0, points, exchange(d_near, NEAR))])
    everyone = lax.all_to_all(jnp.broadcast_to(sums[None], (spaces,) + sums.shape), "space", 0, 0)

    def put(group, *job):
        return place([g[:3] for g in group], quarter, [g[3] for g in group], out, *job)

    out, sums = put(back[0], PLACING, add_rows, (everyone,), sums.shape)
    rows = [exchange(sums, f) for f in (FAR, CROSS, NEAR)]
    out, = put(back[1])
    pen_row = pen[None, :]
    out, field_loss = put(
        back[2], 0, functools.partial(weigh, points * spaces), (pen_row, sums, *rows), pen_row.shape
    )
    return out, field_loss[0]


def solution(mesh):
    return jax.shard_map(
        shards,
        mesh=mesh,
        in_specs=(P("member", None, "space"), P(None, "space"), P("space"), P()),
        out_specs=(P("member", None, "space"), P()),
        check_vma=False,
    )
```

```python
import functools
import math

import jax
import jax.numpy as jnp
from jax import lax
from jax.experimental import pallas as pl
from jax.experimental.pallas import tpu as pltpu
from jax.sharding import PartitionSpec as P

AXES = ("member", "space")
SPLIT = 0.625
LANES = 128
SUBLANES = 8
NEAR, FAR, CROSS = 1, 2, 3
SMALL, LARGE = 4 * 2**20, 16 * 2**20
WORK, PLACING = 400_000, 40 * 10**9
VMEM = pl.BlockSpec(memory_space=pltpu.VMEM)
HBM = pl.BlockSpec(memory_space=pltpu.HBM)
ANY = pl.BlockSpec(memory_space=pl.ANY)


def exchange(block, flip):
    members, spaces = lax.axis_size("member"), lax.axis_size("space")
    pairs = [
        (m * spaces + s, (m ^ flip) * spaces + s) for m in range(members) for s in range(spaces)
    ]
    return lax.ppermute(block, AXES, pairs)


def window(ref, flip, quarter, start, width):
    row = pl.multiple_of((lax.axis_index("member") ^ flip) * quarter, SUBLANES)
    index = (pl.ds(row, quarter), pl.ds(start, width))
    return ref.at[(slice(None),) + index if len(ref.shape) == 3 else index]


def moved(shapes, flops=0):
    size = sum(4 * math.prod(s) for s in shapes)
    return pl.CostEstimate(flops=flops, bytes_accessed=2 * size, transcendentals=0)


def take_kernel(specs, quarter, n_arrays, n_deps, *refs):
    arrays, outs, sems = refs[:n_arrays], refs[n_arrays + n_deps:-1], refs[-1]
    copies = []
    for i, (which, flip, start, width, *member) in enumerate(specs):
        source = window(arrays[which], flip, quarter, start, width)
        if member:
            source = source.at[pl.ds(member[0], 1)]
        copies.append(pltpu.make_async_copy(source, outs[i], sems.at[i]))
    for copy in copies:
        copy.start()
    for copy in copies:
        copy.wait()


def take(specs, quarter, arrays, deps=()):
    shapes = [((1,) if member else arrays[w].shape[:-2]) + (quarter, width) for w, _, _, width, *member in specs]
    return pl.pallas_call(
        functools.partial(take_kernel, specs, quarter, len(arrays), len(deps)),
        out_shape=[jax.ShapeDtypeStruct(s, jnp.float32) for s in shapes],
        in_specs=[HBM] * len(arrays) + [ANY] * len(deps),
        out_specs=[VMEM] * len(specs),
        scratch_shapes=[pltpu.SemaphoreType.DMA((len(specs),))],
        compiler_params=pltpu.CompilerParams(vmem_limit_bytes=SMALL),
        cost_estimate=moved(shapes),
    )(*[pltpu.with_memory_space_constraint(a, pltpu.HBM) for a in arrays], *deps)


def place_kernel(specs, quarter, job, n_more, *refs):
    pieces, more, outs, sems = refs[:len(specs)], refs[len(specs) + 1:][:n_more], refs[len(specs) + 1 + n_more:-1], refs[-1]
    copies = []
    for i, (flip, start, width) in enumerate(specs):
        copies.append(pltpu.make_async_copy(pieces[i], window(outs[0], flip, quarter, start, width), sems.at[i]))
    for copy in copies:
        copy.start()
    if job is not None:
        small = outs[2]
        job(*more, small)
        copies.append(pltpu.make_async_copy(small, outs[1], sems.at[len(specs)]))
        copies[-1].start()
    for copy in copies:
        copy.wait()


def place(specs, quarter, pieces, out, flops=0, job=None, more=(), shape=None):
    shapes = [out.shape] + ([shape] if job else [])
    return pl.pallas_call(
        functools.partial(place_kernel, specs, quarter, job, len(more)),
        out_shape=[jax.ShapeDtypeStruct(s, jnp.float32) for s in shapes],
        in_specs=[VMEM] * len(pieces) + [HBM] + [VMEM] * len(more),
        out_specs=[HBM] * len(shapes),
        scratch_shapes=[pltpu.VMEM(s, jnp.float32) for s in shapes[1:]] + [pltpu.SemaphoreType.DMA((len(specs) + 1,))],
        input_output_aliases={len(pieces): 0},
        compiler_params=pltpu.CompilerParams(vmem_limit_bytes=SMALL),
        cost_estimate=moved([p.shape for p in pieces], flops),
    )(*pieces, out, *more)


def add_rows(rows, total):
    total[...] = jnp.sum(rows[:, 0, :], axis=0, keepdims=True)


def weigh(count, pen, own, far, cross, near, loss):
    total = own[...] + far[...] + cross[...] + near[...]
    loss[...] = pen[...] * total[:, :pen.shape[1]] / count


def score_kernel(scale, weight, start, last, n_before, own, near_0, near_1, far, cross, truth, lat, pen, *refs):
    before, refs = refs[:n_before], refs[n_before:]
    far_out, cross_out, d_near, loss, out, row_sums, d_own, d_far, d_cross, sems = refs
    rows, cols = d_far.shape[1:]
    sources = ((own, 0, start), (own, 1, start), (near_0, 0, start), (near_1, 0, start), (far, 0, 0), (far, 1, 0), (cross, 0, 0), (cross, 1, 0))
    targets = ((d_own, 0), (d_near, start), (d_far, 0), (d_cross, 0))
    homes = ((d_own, window(out, 0, rows, start, cols)), (d_far, far_out), (d_cross, cross_out))
    copies = []
    for row in range(0, rows, SUBLANES):
        r = pl.ds(row, SUBLANES)
        penalty = pen[pl.ds(pl.multiple_of(lax.axis_index("member") * rows + row, SUBLANES), SUBLANES), :]

        def step(i, total):
            def at(shift):
                return pl.ds(pl.multiple_of(i * LANES + shift, LANES), LANES)

            x = [ref[k, r, at(shift)] for ref, k, shift in sources]
            n = len(x)
            y = truth[r, at(start)]
            area = jnp.broadcast_to(lat[:, at(start)], (SUBLANES, LANES))
            signs = [None] * n
            for a in range(n):
                for b in range(a + 1, n):
                    s = jnp.where(x[a] > x[b], 1.0, jnp.where(x[a] < x[b], -1.0, 0.0))
                    signs[a] = s if signs[a] is None else signs[a] + s
                    signs[b] = -s if signs[b] is None else signs[b] - s
            factor = penalty * area
            score = jnp.zeros_like(y)
            for j in range(n):
                e = x[j] - y
                g = jnp.where(e > 0.0, weight, jnp.where(e < 0.0, -weight, 0.0)) - scale * signs[j]
                score = score + e * g
                target, shift = targets[j // 2]
                target[j % 2, r, at(shift)] = factor * g
            return total + area * score

        total = before[1][r, :] if before else jnp.zeros((SUBLANES, LANES), jnp.float32)
        total = lax.fori_loop(0, cols // LANES, step, total, unroll=2)
        loss[r, :] = total
        for i, (source, home) in enumerate(homes):
            copies.append(pltpu.make_async_copy(source.at[:, r], home.at[:, r], sems.at[i, row // SUBLANES]))
            copies[-1].start()
    if last:
        sums = jnp.sum(loss[...], axis=1, keepdims=True)
        field = lax.axis_index("member") * rows + lax.broadcasted_iota(jnp.int32, loss.shape, 0)
        here = lax.broadcasted_iota(jnp.int32, loss.shape, 1) == field
        row_sums[...] = jnp.sum(jnp.where(here, sums, 0.0), axis=0, keepdims=True)
    for copy in copies:
        copy.wait()


def score(scale, weight, start, width, shape, last, own, near, far, cross, truth, lat, pen, *before):
    members, quarter = own.shape[:2]
    block = (members, quarter, width)
    shapes = (block, block, own.shape, (quarter, LANES), shape, (1, LANES))
    return pl.pallas_call(
        functools.partial(score_kernel, scale, weight, start, last, len(before)),
        out_shape=[jax.ShapeDtypeStruct(s, jnp.float32) for s in shapes],
        in_specs=[VMEM] * 8 + [VMEM, VMEM, HBM][:len(before)],
        out_specs=[HBM, HBM, VMEM, VMEM, HBM, VMEM],
        scratch_shapes=[pltpu.VMEM(block, jnp.float32)] * 3 + [pltpu.SemaphoreType.DMA((3, quarter // SUBLANES))],
        input_output_aliases={8: 2, 9: 3, 10: 4} if before else {},
        compiler_params=pltpu.CompilerParams(vmem_limit_bytes=LARGE),
        cost_estimate=pl.CostEstimate(
            flops=WORK * quarter * width, bytes_accessed=20 * quarter * width * 4, transcendentals=0
        ),
    )(own, *near, far, cross, truth, lat, pen, *before)


def shards(x, y, lat, pen):
    members = lax.axis_size("member")
    spaces = lax.axis_size("space")
    samples = x.shape[0] * members
    fields, points = y.shape
    scale = (1.0 - 0.05 / samples) / (samples * (samples - 1))
    quarter = fields // members
    first = int(points * SPLIT)
    chunks = ((0, first), (first, points - first))

    far_cross = [[(0, FAR, start, width), (0, CROSS, start, width)] for start, width in chunks]
    first_sent = take(far_cross[0], quarter, [x])
    second_sent = take(far_cross[1], quarter, [x], first_sent)
    *to_near, own, truth = take(
        [(0, NEAR, 0, points, 0), (0, NEAR, 0, points, 1), (0, 0, 0, points), (1, 0, 0, points)], quarter, [x, y], second_sent
    )
    sent = (first_sent, second_sent)
    far = [exchange(pair[0], FAR) for pair in sent]
    cross = [exchange(pair[1], CROSS) for pair in sent]
    near = [exchange(piece, NEAR) for piece in to_near]
    pen_lanes = jnp.broadcast_to(pen[:, None], (fields, LANES))
    back, before = [], ()
    for c, (start, width) in enumerate(chunks):
        d_far, d_cross, *before, sums = score(
            scale, 1.0 / samples, start, width, x.shape, c == len(chunks) - 1, own, near, far[c], cross[c], truth, lat[None, :], pen_lanes, *before
        )
        back.append([(FAR, start, width, exchange(d_far, FAR)), (CROSS, start, width, exchange(d_cross, CROSS))])
    d_near, loss, out = before
    back.insert(1, [(NEAR, 0, points, exchange(d_near, NEAR))])
    everyone = lax.all_to_all(jnp.broadcast_to(sums[None], (spaces,) + sums.shape), "space", 0, 0)

    def put(group, *job):
        return place([g[:3] for g in group], quarter, [g[3] for g in group], out, *job)

    out, sums = put(back[0], PLACING, add_rows, (everyone,), sums.shape)
    rows = [exchange(sums, f) for f in (FAR, CROSS, NEAR)]
    out, = put(back[1])
    pen_row = pen[None, :]
    out, field_loss = put(
        back[2], 0, functools.partial(weigh, points * spaces), (pen_row, sums, *rows), pen_row.shape
    )
    return out, field_loss[0]


def solution(mesh):
    return jax.shard_map(
        shards,
        mesh=mesh,
        in_specs=(P("member", None, "space"), P(None, "space"), P("space"), P()),
        out_specs=(P("member", None, "space"), P()),
        check_vma=False,
    )
```

```python
import functools
import math

import jax
import jax.numpy as jnp
from jax import lax
from jax.experimental import pallas as pl
from jax.experimental.pallas import tpu as pltpu
from jax.sharding import PartitionSpec as P

AXES = ("member", "space")
SPLIT = 0.625
LANES = 128
SUBLANES = 8
NEAR, FAR, CROSS = 1, 2, 3
SMALL, LARGE = 4 * 2**20, 16 * 2**20
WORK, PLACING = 400_000, 40 * 10**9
VMEM = pl.BlockSpec(memory_space=pltpu.VMEM)
HBM = pl.BlockSpec(memory_space=pltpu.HBM)
ANY = pl.BlockSpec(memory_space=pl.ANY)


def exchange(block, flip):
    members, spaces = lax.axis_size("member"), lax.axis_size("space")
    pairs = [
        (m * spaces + s, (m ^ flip) * spaces + s) for m in range(members) for s in range(spaces)
    ]
    return lax.ppermute(block, AXES, pairs)


def window(ref, flip, quarter, start, width):
    row = pl.multiple_of((lax.axis_index("member") ^ flip) * quarter, SUBLANES)
    index = (pl.ds(row, quarter), pl.ds(start, width))
    return ref.at[(slice(None),) + index if len(ref.shape) == 3 else index]


def moved(shapes, flops=0):
    size = sum(4 * math.prod(s) for s in shapes)
    return pl.CostEstimate(flops=flops, bytes_accessed=2 * size, transcendentals=0)


def take_kernel(specs, quarter, n_arrays, n_deps, *refs):
    arrays, outs, sems = refs[:n_arrays], refs[n_arrays + n_deps:-1], refs[-1]
    copies = []
    for i, (which, flip, start, width, *member) in enumerate(specs):
        source = window(arrays[which], flip, quarter, start, width)
        if member:
            source = source.at[pl.ds(member[0], 1)]
        copies.append(pltpu.make_async_copy(source, outs[i], sems.at[i]))
    for copy in copies:
        copy.start()
    for copy in copies:
        copy.wait()


def take(specs, quarter, arrays, deps=()):
    shapes = [((1,) if member else arrays[w].shape[:-2]) + (quarter, width) for w, _, _, width, *member in specs]
    return pl.pallas_call(
        functools.partial(take_kernel, specs, quarter, len(arrays), len(deps)),
        out_shape=[jax.ShapeDtypeStruct(s, jnp.float32) for s in shapes],
        in_specs=[HBM] * len(arrays) + [ANY] * len(deps),
        out_specs=[VMEM] * len(specs),
        scratch_shapes=[pltpu.SemaphoreType.DMA((len(specs),))],
        compiler_params=pltpu.CompilerParams(vmem_limit_bytes=SMALL),
        cost_estimate=moved(shapes),
    )(*[pltpu.with_memory_space_constraint(a, pltpu.HBM) for a in arrays], *deps)


def place_kernel(specs, quarter, job, n_more, *refs):
    pieces, more, outs, sems = refs[:len(specs)], refs[len(specs) + 1:][:n_more], refs[len(specs) + 1 + n_more:-1], refs[-1]
    copies = []
    for i, (flip, start, width) in enumerate(specs):
        copies.append(pltpu.make_async_copy(pieces[i], window(outs[0], flip, quarter, start, width), sems.at[i]))
    for copy in copies:
        copy.start()
    if job is not None:
        small = outs[2]
        job(*more, small)
        copies.append(pltpu.make_async_copy(small, outs[1], sems.at[len(specs)]))
        copies[-1].start()
    for copy in copies:
        copy.wait()


def place(specs, quarter, pieces, out, flops=0, job=None, more=(), shape=None):
    shapes = [out.shape] + ([shape] if job else [])
    return pl.pallas_call(
        functools.partial(place_kernel, specs, quarter, job, len(more)),
        out_shape=[jax.ShapeDtypeStruct(s, jnp.float32) for s in shapes],
        in_specs=[VMEM] * len(pieces) + [HBM] + [VMEM] * len(more),
        out_specs=[HBM] * len(shapes),
        scratch_shapes=[pltpu.VMEM(s, jnp.float32) for s in shapes[1:]] + [pltpu.SemaphoreType.DMA((len(specs) + 1,))],
        input_output_aliases={len(pieces): 0},
        compiler_params=pltpu.CompilerParams(vmem_limit_bytes=SMALL),
        cost_estimate=moved([p.shape for p in pieces], flops),
    )(*pieces, out, *more)


def add_rows(rows, total):
    total[...] = jnp.sum(rows[:, 0, :], axis=0, keepdims=True)


def weigh(count, pen, own, far, cross, near, loss):
    total = own[...] + far[...] + cross[...] + near[...]
    loss[...] = pen[...] * total[:, :pen.shape[1]] / count


def score_kernel(scale, weight, start, n_before, own, near_0, near_1, far, cross, truth, lat, pen, *refs):
    before, refs = refs[:n_before], refs[n_before:]
    d_far, d_cross, d_near, loss, out, row_sums, d_own, sems = refs
    rows, cols = d_far.shape[1:]
    sources = ((own, 0, start), (own, 1, start), (near_0, 0, start), (near_1, 0, start), (far, 0, 0), (far, 1, 0), (cross, 0, 0), (cross, 1, 0))
    targets = ((d_own, 0), (d_near, start), (d_far, 0), (d_cross, 0))
    homes = ((d_own, window(out, 0, rows, start, cols)),)
    copies = []
    for row in range(0, rows, SUBLANES):
        r = pl.ds(row, SUBLANES)
        penalty = pen[pl.ds(pl.multiple_of(lax.axis_index("member") * rows + row, SUBLANES), SUBLANES), :]

        def step(i, total):
            def at(shift):
                return pl.ds(pl.multiple_of(i * LANES + shift, LANES), LANES)

            x = [ref[k, r, at(shift)] for ref, k, shift in sources]
            n = len(x)
            y = truth[r, at(start)]
            area = jnp.broadcast_to(lat[:, at(start)], (SUBLANES, LANES))
            signs = [None] * n
            for a in range(n):
                for b in range(a + 1, n):
                    s = jnp.where(x[a] > x[b], 1.0, jnp.where(x[a] < x[b], -1.0, 0.0))
                    signs[a] = s if signs[a] is None else signs[a] + s
                    signs[b] = -s if signs[b] is None else signs[b] - s
            factor = penalty * area
            score = jnp.zeros_like(y)
            for j in range(n):
                e = x[j] - y
                g = jnp.where(e > 0.0, weight, jnp.where(e < 0.0, -weight, 0.0)) - scale * signs[j]
                score = score + e * g
                target, shift = targets[j // 2]
                target[j % 2, r, at(shift)] = factor * g
            return total + area * score

        total = before[1][r, :] if before else jnp.zeros((SUBLANES, LANES), jnp.float32)
        total = lax.fori_loop(0, cols // LANES, step, total, unroll=2)
        loss[r, :] = total
        for i, (source, home) in enumerate(homes):
            copies.append(pltpu.make_async_copy(source.at[:, r], home.at[:, r], sems.at[i, row // SUBLANES]))
            copies[-1].start()
    sums = jnp.sum(loss[...], axis=1, keepdims=True)
    field = lax.axis_index("member") * rows + lax.broadcasted_iota(jnp.int32, loss.shape, 0)
    here = lax.broadcasted_iota(jnp.int32, loss.shape, 1) == field
    row_sums[...] = jnp.sum(jnp.where(here, sums, 0.0), axis=0, keepdims=True)
    for copy in copies:
        copy.wait()


def score(scale, weight, start, width, shape, own, near, far, cross, truth, lat, pen, *before):
    members, quarter = own.shape[:2]
    block = (members, quarter, width)
    shapes = (own.shape, (quarter, LANES), shape, (1, LANES))
    return pl.pallas_call(
        functools.partial(score_kernel, scale, weight, start, len(before)),
        out_shape=[jax.ShapeDtypeStruct(s, jnp.float32) for s in (block, block) + shapes],
        in_specs=[VMEM] * 8 + [VMEM, VMEM, HBM][:len(before)],
        out_specs=[VMEM, VMEM, VMEM, VMEM, HBM, VMEM],
        scratch_shapes=[pltpu.VMEM(block, jnp.float32), pltpu.SemaphoreType.DMA((1, quarter // SUBLANES))],
        input_output_aliases={8: 2, 9: 3, 10: 4} if before else {},
        compiler_params=pltpu.CompilerParams(vmem_limit_bytes=LARGE),
        cost_estimate=pl.CostEstimate(
            flops=WORK * quarter * width, bytes_accessed=20 * quarter * width * 4, transcendentals=0
        ),
    )(own, *near, far, cross, truth, lat, pen, *before)


def shards(x, y, lat, pen):
    members = lax.axis_size("member")
    spaces = lax.axis_size("space")
    samples = x.shape[0] * members
    fields, points = y.shape
    scale = (1.0 - 0.05 / samples) / (samples * (samples - 1))
    quarter = fields // members
    first = int(points * SPLIT)
    chunks = ((0, first), (first, points - first))

    far_cross = [[(0, FAR, start, width), (0, CROSS, start, width)] for start, width in chunks]
    first_sent = take(far_cross[0], quarter, [x])
    second_sent = take(far_cross[1], quarter, [x], first_sent)
    *to_near, own, truth = take(
        [(0, NEAR, 0, points, 0), (0, NEAR, 0, points, 1), (0, 0, 0, points), (1, 0, 0, points)], quarter, [x, y], second_sent
    )
    sent = (first_sent, second_sent)
    far = [exchange(pair[0], FAR) for pair in sent]
    cross = [exchange(pair[1], CROSS) for pair in sent]
    near = [exchange(piece, NEAR) for piece in to_near]
    pen_lanes = jnp.broadcast_to(pen[:, None], (fields, LANES))
    back, before = [], ()
    for c, (start, width) in enumerate(chunks):
        d_far, d_cross, *before, sums = score(
            scale, 1.0 / samples, start, width, x.shape, own, near, far[c], cross[c], truth, lat[None, :], pen_lanes, *before
        )
        back.append([(FAR, start, width, exchange(d_far, FAR)), (CROSS, start, width, exchange(d_cross, CROSS))])
    d_near, loss, out = before
    back.insert(1, [(NEAR, 0, points, exchange(d_near, NEAR))])
    everyone = lax.all_to_all(jnp.broadcast_to(sums[None], (spaces,) + sums.shape), "space", 0, 0)

    def put(group, *job):
        return place([g[:3] for g in group], quarter, [g[3] for g in group], out, *job)

    out, sums = put(back[0], PLACING, add_rows, (everyone,), sums.shape)
    rows = [exchange(sums, f) for f in (FAR, CROSS, NEAR)]
    out, = put(back[1])
    pen_row = pen[None, :]
    out, field_loss = put(
        back[2], 0, functools.partial(weigh, points * spaces), (pen_row, sums, *rows), pen_row.shape
    )
    return out, field_loss[0]


def solution(mesh):
    return jax.shard_map(
        shards,
        mesh=mesh,
        in_specs=(P("member", None, "space"), P(None, "space"), P("space"), P()),
        out_specs=(P("member", None, "space"), P()),
        check_vma=False,
    )
```

```python
import functools
import math

import jax
import jax.numpy as jnp
from jax import lax
from jax.experimental import pallas as pl
from jax.experimental.pallas import tpu as pltpu
from jax.sharding import PartitionSpec as P

AXES = ("member", "space")
SPLIT = 0.625
LANES = 128
SUBLANES = 8
NEAR, FAR, CROSS = 1, 2, 3
SMALL, LARGE = 4 * 2**20, 16 * 2**20
WORK, PLACING = 400_000, 40 * 10**9
VMEM = pl.BlockSpec(memory_space=pltpu.VMEM)
HBM = pl.BlockSpec(memory_space=pltpu.HBM)
ANY = pl.BlockSpec(memory_space=pl.ANY)


def exchange(block, flip):
    members, spaces = lax.axis_size("member"), lax.axis_size("space")
    pairs = [
        (m * spaces + s, (m ^ flip) * spaces + s) for m in range(members) for s in range(spaces)
    ]
    return lax.ppermute(block, AXES, pairs)


def window(ref, flip, quarter, start, width):
    row = pl.multiple_of((lax.axis_index("member") ^ flip) * quarter, SUBLANES)
    index = (pl.ds(row, quarter), pl.ds(start, width))
    return ref.at[(slice(None),) + index if len(ref.shape) == 3 else index]


def moved(shapes, flops=0):
    size = sum(4 * math.prod(s) for s in shapes)
    return pl.CostEstimate(flops=flops, bytes_accessed=2 * size, transcendentals=0)


def take_kernel(specs, quarter, n_arrays, n_deps, *refs):
    arrays, outs, sems = refs[:n_arrays], refs[n_arrays + n_deps:-1], refs[-1]
    copies = []
    for i, (which, flip, start, width, *member) in enumerate(specs):
        source = window(arrays[which], flip, quarter, start, width)
        if member:
            source = source.at[pl.ds(member[0], 1)]
        copies.append(pltpu.make_async_copy(source, outs[i], sems.at[i]))
    for copy in copies:
        copy.start()
    for copy in copies:
        copy.wait()


def take(specs, quarter, arrays, deps=()):
    shapes = [((1,) if member else arrays[w].shape[:-2]) + (quarter, width) for w, _, _, width, *member in specs]
    return pl.pallas_call(
        functools.partial(take_kernel, specs, quarter, len(arrays), len(deps)),
        out_shape=[jax.ShapeDtypeStruct(s, jnp.float32) for s in shapes],
        in_specs=[HBM] * len(arrays) + [ANY] * len(deps),
        out_specs=[VMEM] * len(specs),
        scratch_shapes=[pltpu.SemaphoreType.DMA((len(specs),))],
        compiler_params=pltpu.CompilerParams(vmem_limit_bytes=SMALL),
        cost_estimate=moved(shapes),
    )(*[pltpu.with_memory_space_constraint(a, pltpu.HBM) for a in arrays], *deps)


def place_kernel(specs, quarter, job, n_more, *refs):
    pieces, more, outs, sems = refs[:len(specs)], refs[len(specs) + 1:][:n_more], refs[len(specs) + 1 + n_more:-1], refs[-1]
    copies = []
    for i, (flip, start, width) in enumerate(specs):
        copies.append(pltpu.make_async_copy(pieces[i], window(outs[0], flip, quarter, start, width), sems.at[i]))
    for copy in copies:
        copy.start()
    if job is not None:
        small = outs[2]
        job(*more, small)
        copies.append(pltpu.make_async_copy(small, outs[1], sems.at[len(specs)]))
        copies[-1].start()
    for copy in copies:
        copy.wait()


def place(specs, quarter, pieces, out, flops=0, job=None, more=(), shape=None):
    shapes = [out.shape] + ([shape] if job else [])
    return pl.pallas_call(
        functools.partial(place_kernel, specs, quarter, job, len(more)),
        out_shape=[jax.ShapeDtypeStruct(s, jnp.float32) for s in shapes],
        in_specs=[VMEM] * len(pieces) + [HBM] + [VMEM] * len(more),
        out_specs=[HBM] * len(shapes),
        scratch_shapes=[pltpu.VMEM(s, jnp.float32) for s in shapes[1:]] + [pltpu.SemaphoreType.DMA((len(specs) + 1,))],
        input_output_aliases={len(pieces): 0},
        compiler_params=pltpu.CompilerParams(vmem_limit_bytes=SMALL),
        cost_estimate=moved([p.shape for p in pieces], flops),
    )(*pieces, out, *more)


def add_rows(rows, total):
    total[...] = jnp.sum(rows[:, 0, :], axis=0, keepdims=True)


def weigh(count, pen, own, near, loss):
    total = own[...] + near[...]
    loss[...] = pen[...] * total[:, :pen.shape[1]] / count


def score_kernel(scale, weight, start, n_before, own, near_0, near_1, far, cross, truth, lat, pen, *refs):
    before, refs = refs[:n_before], refs[n_before:]
    d_far, d_cross, d_near, loss, out, row_sums, d_own, sems = refs
    rows, cols = d_far.shape[1:]
    sources = ((own, 0, start), (own, 1, start), (near_0, 0, start), (near_1, 0, start), (far, 0, 0), (far, 1, 0), (cross, 0, 0), (cross, 1, 0))
    targets = ((d_own, 0), (d_near, start), (d_far, 0), (d_cross, 0))
    homes = ((d_own, window(out, 0, rows, start, cols)),)
    copies = []
    for row in range(0, rows, SUBLANES):
        r = pl.ds(row, SUBLANES)
        penalty = pen[pl.ds(pl.multiple_of(lax.axis_index("member") * rows + row, SUBLANES), SUBLANES), :]

        def step(i, total):
            def at(shift):
                return pl.ds(pl.multiple_of(i * LANES + shift, LANES), LANES)

            x = [ref[k, r, at(shift)] for ref, k, shift in sources]
            n = len(x)
            y = truth[r, at(start)]
            area = jnp.broadcast_to(lat[:, at(start)], (SUBLANES, LANES))
            signs = [None] * n
            for a in range(n):
                for b in range(a + 1, n):
                    s = jnp.where(x[a] > x[b], 1.0, jnp.where(x[a] < x[b], -1.0, 0.0))
                    signs[a] = s if signs[a] is None else signs[a] + s
                    signs[b] = -s if signs[b] is None else signs[b] - s
            factor = penalty * area
            score = jnp.zeros_like(y)
            for j in range(n):
                e = x[j] - y
                g = jnp.where(e > 0.0, weight, jnp.where(e < 0.0, -weight, 0.0)) - scale * signs[j]
                score = score + e * g
                target, shift = targets[j // 2]
                target[j % 2, r, at(shift)] = factor * g
            return total + area * score

        total = before[1][r, :] if before else jnp.zeros((SUBLANES, LANES), jnp.float32)
        total = lax.fori_loop(0, cols // LANES, step, total, unroll=2)
        loss[r, :] = total
        for i, (source, home) in enumerate(homes):
            copies.append(pltpu.make_async_copy(source.at[:, r], home.at[:, r], sems.at[i, row // SUBLANES]))
            copies[-1].start()
    sums = jnp.sum(loss[...], axis=1, keepdims=True)
    field = lax.axis_index("member") * rows + lax.broadcasted_iota(jnp.int32, loss.shape, 0)
    here = lax.broadcasted_iota(jnp.int32, loss.shape, 1) == field
    row_sums[...] = jnp.sum(jnp.where(here, sums, 0.0), axis=0, keepdims=True)
    for copy in copies:
        copy.wait()


def score(scale, weight, start, width, shape, own, near, far, cross, truth, lat, pen, *before):
    members, quarter = own.shape[:2]
    block = (members, quarter, width)
    shapes = (own.shape, (quarter, LANES), shape, (1, LANES))
    return pl.pallas_call(
        functools.partial(score_kernel, scale, weight, start, len(before)),
        out_shape=[jax.ShapeDtypeStruct(s, jnp.float32) for s in (block, block) + shapes],
        in_specs=[VMEM] * 8 + [VMEM, VMEM, HBM][:len(before)],
        out_specs=[VMEM, VMEM, VMEM, VMEM, HBM, VMEM],
        scratch_shapes=[pltpu.VMEM(block, jnp.float32), pltpu.SemaphoreType.DMA((1, quarter // SUBLANES))],
        input_output_aliases={8: 2, 9: 3, 10: 4} if before else {},
        compiler_params=pltpu.CompilerParams(vmem_limit_bytes=LARGE),
        cost_estimate=pl.CostEstimate(
            flops=WORK * quarter * width, bytes_accessed=20 * quarter * width * 4, transcendentals=0
        ),
    )(own, *near, far, cross, truth, lat, pen, *before)


def shards(x, y, lat, pen):
    members = lax.axis_size("member")
    spaces = lax.axis_size("space")
    samples = x.shape[0] * members
    fields, points = y.shape
    scale = (1.0 - 0.05 / samples) / (samples * (samples - 1))
    quarter = fields // members
    first = int(points * SPLIT)
    chunks = ((0, first), (first, points - first))

    far_cross = [[(0, FAR, start, width), (0, CROSS, start, width)] for start, width in chunks]
    first_sent = take(far_cross[0], quarter, [x])
    second_sent = take(far_cross[1], quarter, [x], first_sent)
    *to_near, own, truth = take(
        [(0, NEAR, 0, points, 0), (0, NEAR, 0, points, 1), (0, 0, 0, points), (1, 0, 0, points)], quarter, [x, y], second_sent
    )
    sent = (first_sent, second_sent)
    far = [exchange(pair[0], FAR) for pair in sent]
    cross = [exchange(pair[1], CROSS) for pair in sent]
    near = [exchange(piece, NEAR) for piece in to_near]
    pen_lanes = jnp.broadcast_to(pen[:, None], (fields, LANES))
    back, before = [], ()
    for c, (start, width) in enumerate(chunks):
        d_far, d_cross, *before, sums = score(
            scale, 1.0 / samples, start, width, x.shape, own, near, far[c], cross[c], truth, lat[None, :], pen_lanes, *before
        )
        back.append([(CROSS, start, width, exchange(d_cross, CROSS)), (FAR, start, width, exchange(d_far, FAR))])
    d_near, loss, out = before
    back.insert(1, [(NEAR, 0, points, exchange(d_near, NEAR))])
    cores = [[m * spaces + s for m in range(core, members, 2) for s in range(spaces)] for core in range(2)]
    copies = jnp.broadcast_to(sums[None], (len(cores[0]),) + sums.shape)
    everyone = lax.all_to_all(copies, AXES, 0, 0, axis_index_groups=cores)

    def put(group, *job):
        return place([g[:3] for g in group], quarter, [g[3] for g in group], out, *job)

    out, sums = put(back[0], PLACING, add_rows, (everyone,), sums.shape)
    near_sums = exchange(sums, NEAR)
    out, = put(back[1])
    pen_row = pen[None, :]
    out, field_loss = put(
        back[2], 0, functools.partial(weigh, points * spaces), (pen_row, sums, near_sums), pen_row.shape
    )
    return out, field_loss[0]


def solution(mesh):
    return jax.shard_map(
        shards,
        mesh=mesh,
        in_specs=(P("member", None, "space"), P(None, "space"), P("space"), P()),
        out_specs=(P("member", None, "space"), P()),
        check_vma=False,
    )
```

```python
import functools
import math

import jax
import jax.numpy as jnp
from jax import lax
from jax.experimental import pallas as pl
from jax.experimental.pallas import tpu as pltpu
from jax.sharding import PartitionSpec as P

AXES = ("member", "space")
LANES = 128
SUBLANES = 8
NEAR, FAR, CROSS = 1, 2, 3
SMALL, LARGE = 4 * 2**20, 16 * 2**20
WORK, PLACING = 400_000, 40 * 10**9
VMEM = pl.BlockSpec(memory_space=pltpu.VMEM)
HBM = pl.BlockSpec(memory_space=pltpu.HBM)
ANY = pl.BlockSpec(memory_space=pl.ANY)


def exchange(block, flip):
    members, spaces = lax.axis_size("member"), lax.axis_size("space")
    pairs = [
        (m * spaces + s, (m ^ flip) * spaces + s) for m in range(members) for s in range(spaces)
    ]
    return lax.ppermute(block, AXES, pairs)


def window(ref, flip, quarter, first, rows):
    row = pl.multiple_of((lax.axis_index("member") ^ flip) * quarter + first, SUBLANES)
    index = (pl.ds(row, rows), slice(None))
    return ref.at[(slice(None),) + index if len(ref.shape) == 3 else index]


def moved(shapes, flops=0):
    size = sum(4 * math.prod(s) for s in shapes)
    return pl.CostEstimate(flops=flops, bytes_accessed=2 * size, transcendentals=0)


def take_kernel(specs, quarter, n_arrays, n_deps, *refs):
    arrays, outs, sems = refs[:n_arrays], refs[n_arrays + n_deps:-1], refs[-1]
    copies = []
    for i, (which, flip, first, rows, *member) in enumerate(specs):
        source = window(arrays[which], flip, quarter, first, rows)
        if member:
            source = source.at[pl.ds(member[0], 1)]
        copies.append(pltpu.make_async_copy(source, outs[i], sems.at[i]))
    for copy in copies:
        copy.start()
    for copy in copies:
        copy.wait()


def take(specs, quarter, arrays, deps=()):
    shapes = [((1,) if member else arrays[w].shape[:-2]) + (rows, arrays[w].shape[-1]) for w, _, _, rows, *member in specs]
    return pl.pallas_call(
        functools.partial(take_kernel, specs, quarter, len(arrays), len(deps)),
        out_shape=[jax.ShapeDtypeStruct(s, jnp.float32) for s in shapes],
        in_specs=[HBM] * len(arrays) + [ANY] * len(deps),
        out_specs=[VMEM] * len(specs),
        scratch_shapes=[pltpu.SemaphoreType.DMA((len(specs),))],
        compiler_params=pltpu.CompilerParams(vmem_limit_bytes=SMALL),
        cost_estimate=moved(shapes),
    )(*[pltpu.with_memory_space_constraint(a, pltpu.HBM) for a in arrays], *deps)


def place_kernel(specs, quarter, job, n_more, *refs):
    pieces, more, outs, sems = refs[:len(specs)], refs[len(specs) + 1:][:n_more], refs[len(specs) + 1 + n_more:-1], refs[-1]
    copies = []
    for i, (flip, first, rows) in enumerate(specs):
        copies.append(pltpu.make_async_copy(pieces[i], window(outs[0], flip, quarter, first, rows), sems.at[i]))
    for copy in copies:
        copy.start()
    if job is not None:
        small = outs[2]
        job(*more, small)
        copies.append(pltpu.make_async_copy(small, outs[1], sems.at[len(specs)]))
        copies[-1].start()
    for copy in copies:
        copy.wait()


def place(specs, quarter, pieces, out, flops=0, job=None, more=(), shape=None):
    shapes = [out.shape] + ([shape] if job else [])
    return pl.pallas_call(
        functools.partial(place_kernel, specs, quarter, job, len(more)),
        out_shape=[jax.ShapeDtypeStruct(s, jnp.float32) for s in shapes],
        in_specs=[VMEM] * len(pieces) + [HBM] + [VMEM] * len(more),
        out_specs=[HBM] * len(shapes),
        scratch_shapes=[pltpu.VMEM(s, jnp.float32) for s in shapes[1:]] + [pltpu.SemaphoreType.DMA((len(specs) + 1,))],
        input_output_aliases={len(pieces): 0},
        compiler_params=pltpu.CompilerParams(vmem_limit_bytes=SMALL),
        cost_estimate=moved([p.shape for p in pieces], flops),
    )(*pieces, out, *more)


def add_rows(rows, total):
    total[...] = jnp.sum(rows[:, 0, :], axis=0, keepdims=True)


def weigh(count, pen, own, near, loss):
    total = own[...] + near[...]
    loss[...] = pen[...] * total[:, :pen.shape[1]] / count


def score_kernel(scale, weight, first, n_before, own, near_0, near_1, far, cross, truth, lat, pen, *refs):
    before, refs = refs[:n_before], refs[n_before:]
    d_far, d_cross, d_near, loss, out, row_sums, d_own, sems = refs
    quarter = d_near.shape[1]
    rows, cols = d_far.shape[1:]
    sources = ((own, 0, first), (own, 1, first), (near_0, 0, first), (near_1, 0, first), (far, 0, 0), (far, 1, 0), (cross, 0, 0), (cross, 1, 0))
    targets = ((d_own, 0), (d_near, first), (d_far, 0), (d_cross, 0))
    homes = ((d_own, window(out, 0, quarter, first, rows)),)
    if before:
        d_near[:, :first, :] = before[0][:, :first, :]
        loss[:first, :] = before[1][:first, :]
    else:
        loss[...] = jnp.zeros_like(loss)
    copies = []
    for row in range(0, rows, SUBLANES):
        r, q = pl.ds(row, SUBLANES), pl.ds(first + row, SUBLANES)
        field = lax.axis_index("member") * quarter + first + row
        penalty = pen[pl.ds(pl.multiple_of(field, SUBLANES), SUBLANES), :]

        def step(i, total):
            c = pl.ds(pl.multiple_of(i * LANES, LANES), LANES)
            x = [ref[k, pl.ds(shift + row, SUBLANES), c] for ref, k, shift in sources]
            n = len(x)
            y = truth[q, c]
            area = jnp.broadcast_to(lat[:, c], (SUBLANES, LANES))
            signs = [None] * n
            for a in range(n):
                for b in range(a + 1, n):
                    s = jnp.where(x[a] > x[b], 1.0, jnp.where(x[a] < x[b], -1.0, 0.0))
                    signs[a] = s if signs[a] is None else signs[a] + s
                    signs[b] = -s if signs[b] is None else signs[b] - s
            factor = penalty * area
            score = jnp.zeros_like(y)
            for j in range(n):
                e = x[j] - y
                g = jnp.where(e > 0.0, weight, jnp.where(e < 0.0, -weight, 0.0)) - scale * signs[j]
                score = score + e * g
                target, shift = targets[j // 2]
                target[j % 2, pl.ds(shift + row, SUBLANES), c] = factor * g
            return total + area * score

        loss[q, :] = lax.fori_loop(0, cols // LANES, step, jnp.zeros((SUBLANES, LANES), jnp.float32), unroll=2)
        for i, (source, home) in enumerate(homes):
            copies.append(pltpu.make_async_copy(source.at[:, r], home.at[:, r], sems.at[i, row // SUBLANES]))
            copies[-1].start()
    sums = jnp.sum(loss[...], axis=1, keepdims=True)
    field = lax.axis_index("member") * quarter + lax.broadcasted_iota(jnp.int32, loss.shape, 0)
    here = lax.broadcasted_iota(jnp.int32, loss.shape, 1) == field
    row_sums[...] = jnp.sum(jnp.where(here, sums, 0.0), axis=0, keepdims=True)
    for copy in copies:
        copy.wait()


def score(scale, weight, first, rows, shape, own, near, far, cross, truth, lat, pen, *before):
    members, quarter = own.shape[:2]
    block = (members, rows, own.shape[2])
    shapes = (own.shape, (quarter, LANES), shape, (1, LANES))
    return pl.pallas_call(
        functools.partial(score_kernel, scale, weight, first, len(before)),
        out_shape=[jax.ShapeDtypeStruct(s, jnp.float32) for s in (block, block) + shapes],
        in_specs=[VMEM] * 8 + [VMEM, VMEM, HBM][:len(before)],
        out_specs=[VMEM, VMEM, VMEM, VMEM, HBM, VMEM],
        scratch_shapes=[pltpu.VMEM(block, jnp.float32), pltpu.SemaphoreType.DMA((1, quarter // SUBLANES))],
        input_output_aliases={8: 2, 9: 3, 10: 4} if before else {},
        compiler_params=pltpu.CompilerParams(vmem_limit_bytes=LARGE),
        cost_estimate=pl.CostEstimate(
            flops=WORK * math.prod(block[1:]), bytes_accessed=80 * math.prod(block[1:]), transcendentals=0
        ),
    )(own, *near, far, cross, truth, lat, pen, *before)


def shards(x, y, lat, pen):
    members = lax.axis_size("member")
    spaces = lax.axis_size("space")
    samples = x.shape[0] * members
    fields, points = y.shape
    scale = (1.0 - 0.05 / samples) / (samples * (samples - 1))
    quarter = fields // members
    split = quarter * 2 // 3 // SUBLANES * SUBLANES
    chunks = ((0, split), (split, quarter - split))

    far_cross = [[(0, FAR, *chunk), (0, CROSS, *chunk)] for chunk in chunks]
    first_sent = take(far_cross[0], quarter, [x])
    second_sent = take(far_cross[1], quarter, [x], first_sent)
    *to_near, own, truth = take(
        [(0, NEAR, 0, quarter, 0), (0, NEAR, 0, quarter, 1), (0, 0, 0, quarter), (1, 0, 0, quarter)], quarter, [x, y], second_sent
    )
    sent = (first_sent, second_sent)
    far = [exchange(pair[0], FAR) for pair in sent]
    cross = [exchange(pair[1], CROSS) for pair in sent]
    near = [exchange(piece, NEAR) for piece in to_near]
    pen_lanes = jnp.broadcast_to(pen[:, None], (fields, LANES))
    back, before = [], ()
    for c, chunk in enumerate(chunks):
        d_far, d_cross, *before, sums = score(
            scale, 1.0 / samples, *chunk, x.shape, own, near, far[c], cross[c], truth, lat[None, :], pen_lanes, *before
        )
        back.append([(CROSS, *chunk, exchange(d_cross, CROSS)), (FAR, *chunk, exchange(d_far, FAR))])
    d_near, loss, out = before
    back.insert(1, [(NEAR, 0, quarter, exchange(d_near, NEAR))])
    cores = [[m * spaces + s for m in range(core, members, 2) for s in range(spaces)] for core in range(2)]
    copies = jnp.broadcast_to(sums[None], (len(cores[0]),) + sums.shape)
    everyone = lax.all_to_all(copies, AXES, 0, 0, axis_index_groups=cores)

    def put(group, *job):
        return place([g[:3] for g in group], quarter, [g[3] for g in group], out, *job)

    out, sums = put(back[0], PLACING, add_rows, (everyone,), sums.shape)
    near_sums = exchange(sums, NEAR)
    out, = put(back[1])
    pen_row = pen[None, :]
    out, field_loss = put(
        back[2], 0, functools.partial(weigh, points * spaces), (pen_row, sums, near_sums), pen_row.shape
    )
    return out, field_loss[0]


def solution(mesh):
    return jax.shard_map(
        shards,
        mesh=mesh,
        in_specs=(P("member", None, "space"), P(None, "space"), P("space"), P()),
        out_specs=(P("member", None, "space"), P()),
        check_vma=False,
    )
```

```python
import functools
import math

import jax
import jax.numpy as jnp
from jax import lax
from jax.experimental import pallas as pl
from jax.experimental.pallas import tpu as pltpu
from jax.sharding import PartitionSpec as P

AXES = ("member", "space")
LANES = 128
SUBLANES = 8
NEAR, FAR, CROSS = 1, 2, 3
SMALL, LARGE = 4 * 2**20, 16 * 2**20
WORK, PLACING = 400_000, 40 * 10**9
VMEM = pl.BlockSpec(memory_space=pltpu.VMEM)
HBM = pl.BlockSpec(memory_space=pltpu.HBM)
ANY = pl.BlockSpec(memory_space=pl.ANY)


def exchange(block, flip):
    members, spaces = lax.axis_size("member"), lax.axis_size("space")
    pairs = [
        (m * spaces + s, (m ^ flip) * spaces + s) for m in range(members) for s in range(spaces)
    ]
    return lax.ppermute(block, AXES, pairs)


def window(ref, flip, quarter, first, rows):
    row = pl.multiple_of((lax.axis_index("member") ^ flip) * quarter + first, SUBLANES)
    index = (pl.ds(row, rows), slice(None))
    return ref.at[(slice(None),) + index if len(ref.shape) == 3 else index]


def moved(shapes, flops=0):
    size = sum(4 * math.prod(s) for s in shapes)
    return pl.CostEstimate(flops=flops, bytes_accessed=2 * size, transcendentals=0)


def take_kernel(specs, quarter, n_arrays, n_deps, *refs):
    arrays, outs, sems = refs[:n_arrays], refs[n_arrays + n_deps:-1], refs[-1]
    copies = []
    for i, (which, flip, first, rows, *member) in enumerate(specs):
        source = window(arrays[which], flip, quarter, first, rows)
        if member:
            source = source.at[pl.ds(member[0], 1)]
        copies.append(pltpu.make_async_copy(source, outs[i], sems.at[i]))
    for copy in copies:
        copy.start()
    for copy in copies:
        copy.wait()


def take(specs, quarter, arrays, deps=()):
    shapes = [((1,) if member else arrays[w].shape[:-2]) + (rows, arrays[w].shape[-1]) for w, _, _, rows, *member in specs]
    return pl.pallas_call(
        functools.partial(take_kernel, specs, quarter, len(arrays), len(deps)),
        out_shape=[jax.ShapeDtypeStruct(s, jnp.float32) for s in shapes],
        in_specs=[HBM] * len(arrays) + [ANY] * len(deps),
        out_specs=[VMEM] * len(specs),
        scratch_shapes=[pltpu.SemaphoreType.DMA((len(specs),))],
        compiler_params=pltpu.CompilerParams(vmem_limit_bytes=SMALL),
        cost_estimate=moved(shapes),
    )(*[pltpu.with_memory_space_constraint(a, pltpu.HBM) for a in arrays], *deps)


def place_kernel(specs, quarter, job, n_more, *refs):
    pieces, more, outs, sems = refs[:len(specs)], refs[len(specs) + 1:][:n_more], refs[len(specs) + 1 + n_more:-1], refs[-1]
    copies = []
    for i, (flip, first, rows) in enumerate(specs):
        copies.append(pltpu.make_async_copy(pieces[i], window(outs[0], flip, quarter, first, rows), sems.at[i]))
    for copy in copies:
        copy.start()
    if job is not None:
        small = outs[2]
        job(*more, small)
        copies.append(pltpu.make_async_copy(small, outs[1], sems.at[len(specs)]))
        copies[-1].start()
    for copy in copies:
        copy.wait()


def place(specs, quarter, pieces, out, flops=0, job=None, more=(), shape=None):
    shapes = [out.shape] + ([shape] if job else [])
    return pl.pallas_call(
        functools.partial(place_kernel, specs, quarter, job, len(more)),
        out_shape=[jax.ShapeDtypeStruct(s, jnp.float32) for s in shapes],
        in_specs=[VMEM] * len(pieces) + [HBM] + [VMEM] * len(more),
        out_specs=[HBM] * len(shapes),
        scratch_shapes=[pltpu.VMEM(s, jnp.float32) for s in shapes[1:]] + [pltpu.SemaphoreType.DMA((len(specs) + 1,))],
        input_output_aliases={len(pieces): 0},
        compiler_params=pltpu.CompilerParams(vmem_limit_bytes=SMALL),
        cost_estimate=moved([p.shape for p in pieces], flops),
    )(*pieces, out, *more)


def add_rows(rows, total):
    total[...] = jnp.sum(rows[:, 0, :], axis=0, keepdims=True)


def weigh(count, pen, own, near, loss):
    total = own[...] + near[...]
    loss[...] = pen[...] * total[:, :pen.shape[1]] / count


def score_kernel(scale, weight, first, n_before, own, near_0, near_1, far, cross, truth, lat, pen, *refs):
    before, refs = refs[:n_before], refs[n_before:]
    d_far, d_cross, d_near, loss, out, row_sums, d_own, sems = refs
    quarter = d_near.shape[1]
    rows, cols = d_far.shape[1:]
    sources = ((own, 0, first), (own, 1, first), (near_0, 0, first), (near_1, 0, first), (far, 0, 0), (far, 1, 0), (cross, 0, 0), (cross, 1, 0))
    targets = ((d_own, 0), (d_near, first), (d_far, 0), (d_cross, 0))
    homes = ((d_own, window(out, 0, quarter, first, rows)),)
    if before:
        d_near[:, :first, :] = before[0][:, :first, :]
        loss[:first, :] = before[1][:first, :]
    else:
        loss[...] = jnp.zeros_like(loss)
    copies = []
    for row in range(0, rows, SUBLANES):
        r, q = pl.ds(row, SUBLANES), pl.ds(first + row, SUBLANES)
        field = lax.axis_index("member") * quarter + first + row
        penalty = pen[pl.ds(pl.multiple_of(field, SUBLANES), SUBLANES), :]

        def step(i, total):
            c = pl.ds(pl.multiple_of(i * LANES, LANES), LANES)
            x = [ref[k, pl.ds(shift + row, SUBLANES), c] for ref, k, shift in sources]
            n = len(x)
            y = truth[q, c]
            area = jnp.broadcast_to(lat[:, c], (SUBLANES, LANES))
            signs = [None] * n
            for a in range(n):
                for b in range(a + 1, n):
                    s = jnp.where(x[a] > x[b], 1.0, jnp.where(x[a] < x[b], -1.0, 0.0))
                    signs[a] = s if signs[a] is None else signs[a] + s
                    signs[b] = -s if signs[b] is None else signs[b] - s
            factor = penalty * area
            score = jnp.zeros_like(y)
            for j in range(n):
                e = x[j] - y
                g = jnp.where(e > 0.0, weight, jnp.where(e < 0.0, -weight, 0.0)) - scale * signs[j]
                score = score + e * g
                target, shift = targets[j // 2]
                target[j % 2, pl.ds(shift + row, SUBLANES), c] = factor * g
            return total + area * score

        loss[q, :] = lax.fori_loop(0, cols // LANES, step, jnp.zeros((SUBLANES, LANES), jnp.float32), unroll=4)
        for i, (source, home) in enumerate(homes):
            copies.append(pltpu.make_async_copy(source.at[:, r], home.at[:, r], sems.at[i, row // SUBLANES]))
            copies[-1].start()
    sums = jnp.sum(loss[...], axis=1, keepdims=True)
    field = lax.axis_index("member") * quarter + lax.broadcasted_iota(jnp.int32, loss.shape, 0)
    here = lax.broadcasted_iota(jnp.int32, loss.shape, 1) == field
    row_sums[...] = jnp.sum(jnp.where(here, sums, 0.0), axis=0, keepdims=True)
    for copy in copies:
        copy.wait()


def score(scale, weight, first, rows, shape, own, near, far, cross, truth, lat, pen, *before):
    members, quarter = own.shape[:2]
    block = (members, rows, own.shape[2])
    shapes = (own.shape, (quarter, LANES), shape, (1, LANES))
    return pl.pallas_call(
        functools.partial(score_kernel, scale, weight, first, len(before)),
        out_shape=[jax.ShapeDtypeStruct(s, jnp.float32) for s in (block, block) + shapes],
        in_specs=[VMEM] * 8 + [VMEM, VMEM, HBM][:len(before)],
        out_specs=[VMEM, VMEM, VMEM, VMEM, HBM, VMEM],
        scratch_shapes=[pltpu.VMEM(block, jnp.float32), pltpu.SemaphoreType.DMA((1, quarter // SUBLANES))],
        input_output_aliases={8: 2, 9: 3, 10: 4} if before else {},
        compiler_params=pltpu.CompilerParams(vmem_limit_bytes=LARGE),
        cost_estimate=pl.CostEstimate(
            flops=WORK * math.prod(block[1:]), bytes_accessed=80 * math.prod(block[1:]), transcendentals=0
        ),
    )(own, *near, far, cross, truth, lat, pen, *before)


def shards(x, y, lat, pen):
    members = lax.axis_size("member")
    spaces = lax.axis_size("space")
    samples = x.shape[0] * members
    fields, points = y.shape
    scale = (1.0 - 0.05 / samples) / (samples * (samples - 1))
    quarter = fields // members
    split = quarter * 2 // 3 // SUBLANES * SUBLANES
    chunks = ((0, split), (split, quarter - split))

    far_cross = [[(0, FAR, *chunk), (0, CROSS, *chunk)] for chunk in chunks]
    first_sent = take(far_cross[0], quarter, [x])
    second_sent = take(far_cross[1], quarter, [x], first_sent)
    *to_near, own, truth = take(
        [(0, NEAR, 0, quarter, 0), (0, NEAR, 0, quarter, 1), (0, 0, 0, quarter), (1, 0, 0, quarter)], quarter, [x, y], second_sent
    )
    sent = (first_sent, second_sent)
    far = [exchange(pair[0], FAR) for pair in sent]
    cross = [exchange(pair[1], CROSS) for pair in sent]
    near = [exchange(piece, NEAR) for piece in to_near]
    pen_lanes = jnp.broadcast_to(pen[:, None], (fields, LANES))
    back, before = [], ()
    for c, chunk in enumerate(chunks):
        d_far, d_cross, *before, sums = score(
            scale, 1.0 / samples, *chunk, x.shape, own, near, far[c], cross[c], truth, lat[None, :], pen_lanes, *before
        )
        back.append([(CROSS, *chunk, exchange(d_cross, CROSS)), (FAR, *chunk, exchange(d_far, FAR))])
    d_near, loss, out = before
    back.insert(1, [(NEAR, 0, quarter, exchange(d_near, NEAR))])
    cores = [[m * spaces + s for m in range(core, members, 2) for s in range(spaces)] for core in range(2)]
    copies = jnp.broadcast_to(sums[None], (len(cores[0]),) + sums.shape)
    everyone = lax.all_to_all(copies, AXES, 0, 0, axis_index_groups=cores)

    def put(group, *job):
        return place([g[:3] for g in group], quarter, [g[3] for g in group], out, *job)

    out, sums = put(back[0], PLACING, add_rows, (everyone,), sums.shape)
    near_sums = exchange(sums, NEAR)
    out, = put(back[1])
    pen_row = pen[None, :]
    out, field_loss = put(
        back[2], 0, functools.partial(weigh, points * spaces), (pen_row, sums, near_sums), pen_row.shape
    )
    return out, field_loss[0]


def solution(mesh):
    return jax.shard_map(
        shards,
        mesh=mesh,
        in_specs=(P("member", None, "space"), P(None, "space"), P("space"), P()),
        out_specs=(P("member", None, "space"), P()),
        check_vma=False,
    )
```
